32 devices in a mesh: feat: 4 (over x, core), rows: 8 (over z, y).
Axes of the slice: x: 2, y: 2, z: 4, core: 2. Of those that a mesh axis runs over, the one named last changes fastest.
Arguments:
- features: bfloat16 [16384, 4096], P('rows', 'feat'), may hold values from -6 to 6
- residual: float32 [16384, 1024], P('rows', 'feat'), may hold values from -8 to 8
- inverse_grams: float32 [4096, 1024], P('feat'), may hold values from -1 to 1, as said below
Outputs:
- increments: bfloat16 [1024, 4096], P(None, 'feat')
- final_residual: float32 [16384, 1024], P('rows', 'feat')
The draws below stay inside these ranges and needn't reach their ends.
Inputs may be any that keep to these rules, and one draw needn't show every extreme that they name: `inverse_grams`: each block of 1024 rows is a symmetric positive definite matrix.
All inputs are finite; a program needn't handle non-finite values.
Results may differ from the reference program's by a relative error of at most 0.0051.
Values may be sent and summed in bfloat16 or wider, within the bound.
No kernel may reach another device: no remote copies, remote signals or barrier semaphores. Data moves between devices by JAX's collectives and lax.ppermute only.
A program may use at most 64 MiB of HBM per device.

```python
import jax
import jax.numpy as jnp
from jax import lax

FB = 1024
LABELS = 1024
ROWS = 16384
NF = 4096
N_FEAT = 4


def draw_inverse_grams(key, part):
    count = NF // FB
    noise = jax.random.normal(key, (count, FB, FB), jnp.float32)
    symmetric = (noise + jnp.swapaxes(noise, 1, 2)) / jnp.sqrt(2.0 * FB)
    identity = jnp.eye(FB, dtype=jnp.float32)
    blocks_out = (identity[None, :, :] + 0.3 * symmetric) * (1.0 / ROWS)
    return blocks_out.reshape(NF, FB)


def block_levels(key, shape, shards, least, high):
    loudness = 1.0
    for axis_at, shards_of in shards:
        steps = jax.random.uniform(jax.random.fold_in(jax.random.fold_in(key, 6), axis_at), (shards_of,), jnp.float32, least / len(shards), high / len(shards))
        loudness = loudness * jnp.repeat(jnp.exp(steps), shape[axis_at] // shards_of).reshape((-1,) + (1,) * (len(shape) - 1 - axis_at))
    return loudness


def normal_values(own_key, shape, scale, most, pieces=(), kind=jnp.bfloat16):
    factor_of = block_levels(own_key, shape, pieces, -0.22, 0.18) if pieces else 1.0
    values = jax.random.normal(own_key, shape, jnp.float32) * scale * factor_of
    return jnp.minimum(jnp.maximum(values, -most), most).astype(kind)


def setup_inputs(seed: int = 0) -> dict:
    seeds = jax.random.split(jax.random.key(seed), 4)
    return {
        "features": normal_values(seeds[0], (ROWS, NF), 1.0, 6.0, ((0, 8), (1, 4))),
        "residual": normal_values(seeds[1], (ROWS, LABELS), 1.0, 8.0, ((0, 8), (1, 4)), jnp.float32),
        "inverse_grams": draw_inverse_grams(jax.random.fold_in(seeds[3], 71), 0),
    }


def reference(features, residual, inverse_grams):
    block_count = N_FEAT
    width = LABELS // block_count
    increments = jnp.zeros((LABELS, NF), jnp.bfloat16)
    finished = []
    for front in range(block_count):
        current = residual[:, front * width:(front + 1) * width]
        for visit in range(block_count):
            block = (front + visit) % block_count
            block_feats = features[:, block * FB:(block + 1) * FB]
            rounded = current.astype(jnp.bfloat16)
            projected = jnp.dot(rounded.T, block_feats, preferred_element_type=jnp.float32)
            inverse = inverse_grams[block * FB:(block + 1) * FB, :]
            update = jnp.dot(projected, inverse.T, precision=lax.Precision.HIGHEST).astype(jnp.bfloat16)
            current = current - jnp.dot(block_feats, update.T, preferred_element_type=jnp.float32)
            increments = increments.at[front * width:(front + 1) * width, block * FB:(block + 1) * FB].set(update)
        finished.append(current)
    return increments, jnp.concatenate(finished, axis=1)
```

```python
import jax
import jax.numpy as jnp
from jax import lax
from jax.sharding import PartitionSpec as P

BF16 = jnp.bfloat16
F32 = jnp.float32


def send(value, axis, pairs):
    return lax.ppermute(value, axis, pairs)


def on_device(features, residual, inverse_grams):
    blocks = lax.axis_size("feat")
    block_id = lax.axis_index("feat")
    shards = lax.axis_size("rows")
    shard_id = lax.axis_index("rows")
    width = residual.shape[1]
    feat_width = features.shape[1]
    inner = 2
    outer = shards // inner
    inner_id = shard_id % inner
    outer_id = shard_id // inner
    half = width // inner
    piece = half // outer
    next_block = [(source, (source + 1) % blocks) for source in range(blocks)]
    partner = [(source, source ^ 1) for source in range(shards)]

    def outer_step(step):
        return [
            (o * inner + i, ((o + step) % outer) * inner + i)
            for o in range(outer)
            for i in range(inner)
        ]

    inverse_high = inverse_grams.astype(BF16)
    inverse_low = (inverse_grams - inverse_high.astype(F32)).astype(BF16)

    def project(current):
        return lax.dot_general(
            current, features, (((0,), (0,)), ((), ())), preferred_element_type=F32
        )

    def apply_inverse(projected):
        high = projected.astype(BF16)
        low = (projected - high.astype(F32)).astype(BF16)
        dims = (((1,), (1,)), ((), ()))
        dot = lambda a, b: lax.dot_general(a, b, dims, preferred_element_type=F32)
        both = dot(jnp.concatenate([high, low], 0), inverse_high)
        return (both[: high.shape[0]] + both[high.shape[0]:] + dot(high, inverse_low)).astype(BF16)

    def subtract(current, update):
        change = lax.dot_general(
            features, update, (((1,), (1,)), ((), ())), preferred_element_type=F32
        )
        return current.astype(F32) - change

    def reduce_outer(total):
        parts = [lax.dynamic_slice_in_dim(total, outer_id * piece, piece, 0)]
        for step in range(1, outer):
            target = (outer_id + step) % outer
            out = lax.dynamic_slice_in_dim(total, target * piece, piece, 0).astype(BF16)
            parts.append(send(out, "rows", outer_step(step)).astype(F32))
        return sum(parts[1:], parts[0])

    def gather_outer(update):
        full = jnp.zeros((half, feat_width), BF16)
        full = lax.dynamic_update_slice_in_dim(full, update, outer_id * piece, 0)
        for step in range(1, outer):
            source = (outer_id - step) % outer
            got = send(update, "rows", outer_step(step))
            full = lax.dynamic_update_slice_in_dim(full, got, source * piece, 0)
        return full

    increments = jnp.zeros((width * blocks, feat_width), BF16)
    halves = [lax.dynamic_slice_in_dim(residual, s * half, half, 1) for s in (1 - inner_id, inner_id)]
    lead = 1 - inner_id
    for visit in range(blocks):
        front = (block_id - visit) % blocks
        away, home = halves
        arrived = send(project(away.astype(BF16)).astype(BF16), "rows", partner)
        total = project(home.astype(BF16)) + arrived.astype(F32)
        update_home = gather_outer(apply_inverse(reduce_outer(total)))
        update_away = send(update_home, "rows", partner)
        home = subtract(home, update_home)
        away = subtract(away, update_away)
        start = front * width
        increments = lax.dynamic_update_slice_in_dim(increments, update_home, start + (1 - lead) * half, 0)
        increments = lax.dynamic_update_slice_in_dim(increments, update_away, start + lead * half, 0)
        halves = [send(part.astype(BF16), "feat", next_block) for part in (home, away)]
        lead = 1 - lead
    low = lead == 0
    first = jnp.where(low, halves[0], halves[1])
    second = jnp.where(low, halves[1], halves[0])
    return increments, jnp.concatenate([first, second], 1).astype(F32)


def solution(mesh):
    placed = (P("rows", "feat"), P("rows", "feat"), P("feat", None))
    return jax.shard_map(
        on_device,
        mesh=mesh,
        in_specs=placed,
        out_specs=(P(None, "feat"), P("rows", "feat")),
        check_vma=False,
    )
```

```python
import jax
import jax.numpy as jnp
from jax import lax
from jax.sharding import PartitionSpec as P

BF16 = jnp.bfloat16
F32 = jnp.float32


def split_high_low(value):
    high = lax.reduce_precision(value, 8, 7)
    return high.astype(BF16), (value - high).astype(BF16)


def on_device(features, residual, inverse_grams):
    blocks = lax.axis_size("feat")
    block_id = lax.axis_index("feat")
    shards = lax.axis_size("rows")
    shard_id = lax.axis_index("rows")
    width = residual.shape[1]
    feat_width = features.shape[1]
    inner = 2
    outer = shards // inner
    inner_id = shard_id % inner
    outer_id = shard_id // inner
    half = width // inner
    piece = half // outer
    next_block = [(source, (source + 1) % blocks) for source in range(blocks)]
    partner = [(source, source ^ 1) for source in range(shards)]
    outer_groups = [[o * inner + i for o in range(outer)] for i in range(inner)]
    direct = outer == 4

    def outer_step(step):
        return [(o * inner + i, (o ^ step) * inner + i) for o in range(outer) for i in range(inner)]

    def project(current):
        return lax.dot_general(
            current, features, (((1,), (0,)), ((), ())), preferred_element_type=F32
        )

    def apply_inverse(projected, inverse_high, inverse_low):
        high, low = split_high_low(projected)
        dims = (((1,), (1,)), ((), ()))
        dot = lambda a, b: lax.dot_general(a, b, dims, preferred_element_type=F32)
        both = dot(jnp.concatenate([high, low], 0), inverse_high)
        return (both[: high.shape[0]] + both[high.shape[0]:] + dot(high, inverse_low)).astype(BF16)

    def subtract(current, update):
        change = lax.dot_general(
            update, features, (((1,), (1,)), ((), ())), preferred_element_type=F32
        )
        return current.astype(F32) - change

    def reduce_outer(total):
        if not direct:
            parts = lax.all_to_all(
                total.astype(BF16), "rows", 0, 0, tiled=True, axis_index_groups=outer_groups
            )
            return jnp.sum(parts.reshape(outer, piece, feat_width).astype(F32), axis=0)
        parts = [lax.dynamic_slice_in_dim(total, outer_id * piece, piece, 0)]
        for step in range(outer - 1, 0, -1):
            out = lax.dynamic_slice_in_dim(total, (outer_id ^ step) * piece, piece, 0)
            parts.append(lax.ppermute(out.astype(BF16), "rows", outer_step(step)).astype(F32))
        return sum(parts[1:], parts[0])

    def gather_outer(update):
        if not direct:
            repeated = jnp.concatenate([update] * outer, 0)
            return lax.all_to_all(
                repeated, "rows", 0, 0, tiled=True, axis_index_groups=outer_groups
            )
        full = jnp.zeros((half, feat_width), BF16)
        full = lax.dynamic_update_slice_in_dim(full, update, outer_id * piece, 0)
        for step in range(outer - 1, 0, -1):
            got = lax.ppermute(update, "rows", outer_step(step))
            full = lax.dynamic_update_slice_in_dim(full, got, (outer_id ^ step) * piece, 0)
        return full

    increments = jnp.zeros((width * blocks, feat_width), BF16)
    halves = [
        lax.dynamic_slice_in_dim(residual, s * half, half, 1).T for s in (1 - inner_id, inner_id)
    ]
    lead = 1 - inner_id
    for visit in range(blocks):
        front = (block_id - visit) % blocks
        away, home = halves
        arrived = lax.ppermute(project(away.astype(BF16)).astype(BF16), "rows", partner)
        kept = project(home.astype(BF16))
        if visit == 0:
            inverse_high, inverse_low = split_high_low(inverse_grams)
        arrived, kept = lax.optimization_barrier((arrived, kept))
        total = kept + arrived.astype(F32)
        update_home = gather_outer(apply_inverse(reduce_outer(total), inverse_high, inverse_low))
        update_away = lax.ppermute(update_home, "rows", partner)
        home = subtract(home, update_home)
        away = subtract(away, update_away)
        start = front * width
        increments = lax.dynamic_update_slice_in_dim(
            increments, update_home, start + (1 - lead) * half, 0
        )
        increments = lax.dynamic_update_slice_in_dim(
            increments, update_away, start + lead * half, 0
        )
        halves = [lax.ppermute(part.astype(BF16), "feat", next_block) for part in (home, away)]
        lead = 1 - lead
    first = jnp.where(lead == 0, halves[0], halves[1])
    second = jnp.where(lead == 0, halves[1], halves[0])
    return increments, jnp.concatenate([first, second], 0).astype(F32).T


def solution(mesh):
    placed = (P("rows", "feat"), P("rows", "feat"), P("feat", None))
    return jax.shard_map(
        on_device,
        mesh=mesh,
        in_specs=placed,
        out_specs=(P(None, "feat"), P("rows", "feat")),
        check_vma=False,
    )
```

```python
import functools

import jax
import jax.numpy as jnp
from jax import lax
from jax.experimental import pallas as pl
from jax.experimental.pallas import tpu as pltpu
from jax.sharding import PartitionSpec as P

BF16 = jnp.bfloat16
F32 = jnp.float32


def split_high_low(value):
    high = lax.reduce_precision(value, 8, 7)
    return high.astype(BF16), (value - high).astype(BF16)


CHUNK = 1024
LANES = 128
FIRST_VMEM = 56 * 1024 * 1024
SCATTER_VMEM = 12 * 1024 * 1024


def first_kernel(lead_ref, away_ref, home_ref, x_ref, term_ref, kept_ref, away_out, home_out, acc):
    step = pl.program_id(0)
    half = away_ref.shape[1]
    away = away_ref[...].T
    home = home_ref[...].T
    away_out[...] = away
    home_out[...] = home
    both = jnp.concatenate([away, home], 0).astype(BF16)
    product = jnp.dot(both, x_ref[...], preferred_element_type=F32)

    @pl.when(step == 0)
    def _():
        acc[...] = product

    @pl.when(step > 0)
    def _():
        acc[...] += product

    @pl.when(step == pl.num_programs(0) - 1)
    def _():
        term_ref[...] = acc[:half, :].astype(BF16)
        kept_ref[...] = acc[half:, :]


def first_projection(features, residual, lead):
    rows, feat_width = features.shape
    half = residual.shape[1] // 2
    return pl.pallas_call(
        first_kernel,
        out_shape=(
            jax.ShapeDtypeStruct((half, feat_width), BF16),
            jax.ShapeDtypeStruct((half, feat_width), F32),
            jax.ShapeDtypeStruct((half, rows), F32),
            jax.ShapeDtypeStruct((half, rows), F32),
        ),
        grid_spec=pltpu.PrefetchScalarGridSpec(
            num_scalar_prefetch=1,
            grid=(rows // CHUNK,),
            in_specs=[
                pl.BlockSpec((CHUNK, half), lambda i, lead: (i, lead[0])),
                pl.BlockSpec((CHUNK, half), lambda i, lead: (i, 1 - lead[0])),
                pl.BlockSpec((CHUNK, feat_width), lambda i, lead: (i, 0)),
            ],
            out_specs=[
                pl.BlockSpec((half, feat_width), lambda i, lead: (0, 0)),
                pl.BlockSpec((half, feat_width), lambda i, lead: (0, 0)),
                pl.BlockSpec((half, CHUNK), lambda i, lead: (0, i)),
                pl.BlockSpec((half, CHUNK), lambda i, lead: (0, i)),
            ],
            scratch_shapes=[pltpu.VMEM((2 * half, feat_width), F32)],
        ),
        compiler_params=pltpu.CompilerParams(vmem_limit_bytes=FIRST_VMEM),
        cost_estimate=pl.CostEstimate(
            flops=4 * rows * half * feat_width,
            bytes_accessed=2 * rows * feat_width + 16 * rows * half + 6 * half * feat_width,
            transcendentals=0,
        ),
    )(lead.reshape(1), residual, residual, features)


def scatter_kernel(pieces, start_ref, *refs):
    updates, out_ref = refs[:pieces], refs[pieces]
    height = updates[0].shape[0]
    for at in range(pieces):
        rows = pl.ds(pl.multiple_of(start_ref[at] * height, height), height)
        out_ref[rows, :] = updates[at][...]


def scatter_rows(updates, starts):
    pieces = len(updates)
    height, feat_width = updates[0].shape
    whole = lambda i, starts: (0, 0)
    return pl.pallas_call(
        functools.partial(scatter_kernel, pieces),
        out_shape=jax.ShapeDtypeStruct((pieces * height, feat_width), BF16),
        grid_spec=pltpu.PrefetchScalarGridSpec(
            num_scalar_prefetch=1,
            grid=(1,),
            in_specs=[pl.BlockSpec((height, feat_width), whole)] * pieces,
            out_specs=pl.BlockSpec((pieces * height, feat_width), whole),
        ),
        compiler_params=pltpu.CompilerParams(vmem_limit_bytes=SCATTER_VMEM),
        cost_estimate=pl.CostEstimate(
            flops=0, bytes_accessed=4 * pieces * height * feat_width, transcendentals=0
        ),
    )(jnp.stack(starts).astype(jnp.int32), *updates)


def on_device(features, residual, inverse_grams):
    blocks = lax.axis_size("feat")
    block_id = lax.axis_index("feat")
    shards = lax.axis_size("rows")
    shard_id = lax.axis_index("rows")
    width = residual.shape[1]
    feat_width = features.shape[1]
    inner = 2
    outer = shards // inner
    inner_id = shard_id % inner
    outer_id = shard_id // inner
    half = width // inner
    piece = half // outer
    next_block = [(source, (source + 1) % blocks) for source in range(blocks)]
    partner = [(source, source ^ 1) for source in range(shards)]
    outer_groups = [[o * inner + i for o in range(outer)] for i in range(inner)]
    direct = outer == 4

    def outer_step(step):
        return [(o * inner + i, (o ^ step) * inner + i) for o in range(outer) for i in range(inner)]

    def project(current):
        return lax.dot_general(
            current, features, (((1,), (0,)), ((), ())), preferred_element_type=F32
        )

    def apply_inverse(projected, inverse_high, inverse_low):
        high, low = split_high_low(projected)
        dims = (((1,), (1,)), ((), ()))
        dot = lambda a, b: lax.dot_general(a, b, dims, preferred_element_type=F32)
        both = dot(jnp.concatenate([high, low], 0), inverse_high)
        return (both[: high.shape[0]] + both[high.shape[0]:] + dot(high, inverse_low)).astype(BF16)

    def subtract(current, update):
        change = lax.dot_general(
            update, features, (((1,), (1,)), ((), ())), preferred_element_type=F32
        )
        return current.astype(F32) - change

    def reduce_outer(total):
        if not direct:
            parts = lax.all_to_all(
                total.astype(BF16), "rows", 0, 0, tiled=True, axis_index_groups=outer_groups
            )
            return jnp.sum(parts.reshape(outer, piece, feat_width).astype(F32), axis=0)
        parts = [lax.dynamic_slice_in_dim(total, outer_id * piece, piece, 0)]
        for step in range(outer - 1, 0, -1):
            out = lax.dynamic_slice_in_dim(total, (outer_id ^ step) * piece, piece, 0)
            parts.append(lax.ppermute(out.astype(BF16), "rows", outer_step(step)).astype(F32))
        return sum(parts[1:], parts[0])

    def gather_outer(update):
        if not direct:
            repeated = jnp.concatenate([update] * outer, 0)
            return lax.all_to_all(
                repeated, "rows", 0, 0, tiled=True, axis_index_groups=outer_groups
            )
        full = jnp.zeros((half, feat_width), BF16)
        full = lax.dynamic_update_slice_in_dim(full, update, outer_id * piece, 0)
        for step in range(outer - 1, 0, -1):
            got = lax.ppermute(update, "rows", outer_step(step))
            full = lax.dynamic_update_slice_in_dim(full, got, (outer_id ^ step) * piece, 0)
        return full

    updates, starts = [], []
    kernels = half % LANES == 0 and features.shape[0] % CHUNK == 0 and feat_width % LANES == 0
    if kernels:
        term, kept, *halves = first_projection(features, residual, 1 - inner_id)
    else:
        halves = [
            lax.dynamic_slice_in_dim(residual, s * half, half, 1).T
            for s in (1 - inner_id, inner_id)
        ]
    lead = 1 - inner_id
    for visit in range(blocks):
        front = (block_id - visit) % blocks
        away, home = halves
        if visit > 0 or not kernels:
            term = project(away.astype(BF16)).astype(BF16)
            kept = project(home.astype(BF16))
        arrived = lax.ppermute(term, "rows", partner)
        if visit == 0:
            inverse_high, inverse_low = split_high_low(inverse_grams)
            arrived, kept, inverse_high, inverse_low = lax.optimization_barrier(
                (arrived, kept, inverse_high, inverse_low)
            )
        else:
            arrived, kept = lax.optimization_barrier((arrived, kept))
        total = kept + arrived.astype(F32)
        update_home = gather_outer(apply_inverse(reduce_outer(total), inverse_high, inverse_low))
        update_away = lax.ppermute(update_home, "rows", partner)
        home = subtract(home, update_home)
        away = subtract(away, update_away)
        updates += [update_home, update_away]
        starts += [front * inner + (1 - lead), front * inner + lead]
        halves = [lax.ppermute(part.astype(BF16), "feat", next_block) for part in (home, away)]
        lead = 1 - lead
    if kernels:
        increments = scatter_rows(updates, starts)
    else:
        increments = jnp.zeros((width * blocks, feat_width), BF16)
        for update, start in zip(updates, starts):
            increments = lax.dynamic_update_slice_in_dim(increments, update, start * half, 0)
    first = jnp.where(lead == 0, halves[0], halves[1])
    second = jnp.where(lead == 0, halves[1], halves[0])
    return increments, jnp.concatenate([first, second], 0).astype(F32).T


def solution(mesh):
    placed = (P("rows", "feat"), P("rows", "feat"), P("feat", None))
    return jax.shard_map(
        on_device,
        mesh=mesh,
        in_specs=placed,
        out_specs=(P(None, "feat"), P("rows", "feat")),
        check_vma=False,
    )
```

```python
import functools

import jax
import jax.numpy as jnp
from jax import lax
from jax.experimental import pallas as pl
from jax.experimental.pallas import tpu as pltpu
from jax.sharding import PartitionSpec as P

BF16 = jnp.bfloat16
F32 = jnp.float32


def split_high_low(value):
    high = lax.reduce_precision(value, 8, 7)
    return high.astype(BF16), (value - high).astype(BF16)


CHUNK = 1024
LANES = 128
TURN_CHUNK = 512
FIRST_VMEM = 56 * 1024 * 1024
SCATTER_VMEM = 12 * 1024 * 1024


def first_kernel(lead_ref, away_ref, home_ref, x_ref, term_ref, kept_ref, away_out, home_out, acc):
    step = pl.program_id(0)
    half = away_ref.shape[1]
    away = away_ref[...].T
    home = home_ref[...].T
    away_out[...] = away
    home_out[...] = home
    both = jnp.concatenate([away, home], 0).astype(BF16)
    product = jnp.dot(both, x_ref[...], preferred_element_type=F32)

    @pl.when(step == 0)
    def _():
        acc[...] = product

    @pl.when(step > 0)
    def _():
        acc[...] += product

    @pl.when(step == pl.num_programs(0) - 1)
    def _():
        term_ref[...] = acc[:half, :].astype(BF16)
        kept_ref[...] = acc[half:, :]


def first_projection(features, residual, lead):
    rows, feat_width = features.shape
    half = residual.shape[1] // 2
    return pl.pallas_call(
        first_kernel,
        out_shape=(
            jax.ShapeDtypeStruct((half, feat_width), BF16),
            jax.ShapeDtypeStruct((half, feat_width), F32),
            jax.ShapeDtypeStruct((half, rows), F32),
            jax.ShapeDtypeStruct((half, rows), F32),
        ),
        grid_spec=pltpu.PrefetchScalarGridSpec(
            num_scalar_prefetch=1,
            grid=(rows // CHUNK,),
            in_specs=[
                pl.BlockSpec((CHUNK, half), lambda i, lead: (i, lead[0])),
                pl.BlockSpec((CHUNK, half), lambda i, lead: (i, 1 - lead[0])),
                pl.BlockSpec((CHUNK, feat_width), lambda i, lead: (i, 0)),
            ],
            out_specs=[
                pl.BlockSpec((half, feat_width), lambda i, lead: (0, 0)),
                pl.BlockSpec((half, feat_width), lambda i, lead: (0, 0)),
                pl.BlockSpec((half, CHUNK), lambda i, lead: (0, i)),
                pl.BlockSpec((half, CHUNK), lambda i, lead: (0, i)),
            ],
            scratch_shapes=[pltpu.VMEM((2 * half, feat_width), F32)],
        ),
        compiler_params=pltpu.CompilerParams(vmem_limit_bytes=FIRST_VMEM),
        cost_estimate=pl.CostEstimate(
            flops=4 * rows * half * feat_width,
            bytes_accessed=2 * rows * feat_width + 16 * rows * half + 6 * half * feat_width,
            transcendentals=0,
        ),
    )(lead.reshape(1), residual, residual, features)


def turn_kernel(x_ref, out_ref):
    out_ref[...] = x_ref[...].T


def turn(features):
    rows, feat_width = features.shape
    return pl.pallas_call(
        turn_kernel,
        out_shape=jax.ShapeDtypeStruct((feat_width, rows), features.dtype),
        grid=(rows // TURN_CHUNK,),
        in_specs=[pl.BlockSpec((TURN_CHUNK, feat_width), lambda i: (i, 0))],
        out_specs=pl.BlockSpec((feat_width, TURN_CHUNK), lambda i: (0, i)),
        compiler_params=pltpu.CompilerParams(vmem_limit_bytes=SCATTER_VMEM),
        cost_estimate=pl.CostEstimate(
            flops=0, bytes_accessed=4 * rows * feat_width, transcendentals=0
        ),
    )(features)


def scatter_kernel(pieces, start_ref, *refs):
    updates, out_ref = refs[:pieces], refs[pieces]
    height = updates[0].shape[0]
    for at in range(pieces):
        rows = pl.ds(pl.multiple_of(start_ref[at] * height, height), height)
        out_ref[rows, :] = updates[at][...]


def scatter_rows(updates, starts):
    pieces = len(updates)
    height, feat_width = updates[0].shape
    whole = lambda i, starts: (0, 0)
    return pl.pallas_call(
        functools.partial(scatter_kernel, pieces),
        out_shape=jax.ShapeDtypeStruct((pieces * height, feat_width), BF16),
        grid_spec=pltpu.PrefetchScalarGridSpec(
            num_scalar_prefetch=1,
            grid=(1,),
            in_specs=[pl.BlockSpec((height, feat_width), whole)] * pieces,
            out_specs=pl.BlockSpec((pieces * height, feat_width), whole),
        ),
        compiler_params=pltpu.CompilerParams(vmem_limit_bytes=SCATTER_VMEM),
        cost_estimate=pl.CostEstimate(
            flops=0, bytes_accessed=4 * pieces * height * feat_width, transcendentals=0
        ),
    )(jnp.stack(starts).astype(jnp.int32), *updates)


def place_kernel(place_ref, part_ref, *refs):
    refs[-1][...] = part_ref[...].astype(F32).T


def place_columns(part, place, base):
    half, rows = part.shape
    operands = (part,) if base is None else (part, base)
    in_specs = [pl.BlockSpec((half, CHUNK), lambda i, place: (0, i))]
    if base is not None:
        in_specs.append(pl.BlockSpec(memory_space=pl.ANY))
    return pl.pallas_call(
        place_kernel,
        out_shape=jax.ShapeDtypeStruct((rows, 2 * half), F32),
        grid_spec=pltpu.PrefetchScalarGridSpec(
            num_scalar_prefetch=1,
            grid=(rows // CHUNK,),
            in_specs=in_specs,
            out_specs=pl.BlockSpec((CHUNK, half), lambda i, place: (i, place[0])),
        ),
        input_output_aliases={} if base is None else {2: 0},
        compiler_params=pltpu.CompilerParams(vmem_limit_bytes=SCATTER_VMEM),
        cost_estimate=pl.CostEstimate(
            flops=0, bytes_accessed=6 * rows * half, transcendentals=0
        ),
    )(place.reshape(1).astype(jnp.int32), *operands)


def on_device(features, residual, inverse_grams):
    blocks = lax.axis_size("feat")
    block_id = lax.axis_index("feat")
    shards = lax.axis_size("rows")
    shard_id = lax.axis_index("rows")
    width = residual.shape[1]
    feat_width = features.shape[1]
    inner = 2
    outer = shards // inner
    inner_id = shard_id % inner
    outer_id = shard_id // inner
    half = width // inner
    piece = half // outer
    next_block = [(source, (source + 1) % blocks) for source in range(blocks)]
    partner = [(source, source ^ 1) for source in range(shards)]
    outer_groups = [[o * inner + i for o in range(outer)] for i in range(inner)]
    direct = outer == 4

    def outer_step(step):
        return [(o * inner + i, (o ^ step) * inner + i) for o in range(outer) for i in range(inner)]

    def project(current):
        return lax.dot_general(
            current, features, (((1,), (0,)), ((), ())), preferred_element_type=F32
        )

    def apply_inverse(projected, inverse_high, inverse_low):
        high, low = split_high_low(projected)
        dims = (((1,), (1,)), ((), ()))
        dot = lambda a, b: lax.dot_general(a, b, dims, preferred_element_type=F32)
        both = dot(jnp.concatenate([high, low], 0), inverse_high)
        return (both[: high.shape[0]] + both[high.shape[0]:] + dot(high, inverse_low)).astype(BF16)

    def subtract(current, update):
        change = lax.dot_general(
            update, turned, (((1,), (0,)), ((), ())), preferred_element_type=F32
        )
        return current.astype(F32) - change

    def reduce_outer(total):
        if not direct:
            parts = lax.all_to_all(
                total.astype(BF16), "rows", 0, 0, tiled=True, axis_index_groups=outer_groups
            )
            return jnp.sum(parts.reshape(outer, piece, feat_width).astype(F32), axis=0)
        parts = [lax.dynamic_slice_in_dim(total, outer_id * piece, piece, 0)]
        for step in range(outer - 1, 0, -1):
            out = lax.dynamic_slice_in_dim(total, (outer_id ^ step) * piece, piece, 0)
            parts.append(lax.ppermute(out.astype(BF16), "rows", outer_step(step)).astype(F32))
        return sum(parts[1:], parts[0])

    def gather_outer(update):
        if not direct:
            repeated = jnp.concatenate([update] * outer, 0)
            return lax.all_to_all(
                repeated, "rows", 0, 0, tiled=True, axis_index_groups=outer_groups
            )
        full = jnp.zeros((half, feat_width), BF16)
        full = lax.dynamic_update_slice_in_dim(full, update, outer_id * piece, 0)
        for step in range(outer - 1, 0, -1):
            got = lax.ppermute(update, "rows", outer_step(step))
            full = lax.dynamic_update_slice_in_dim(full, got, (outer_id ^ step) * piece, 0)
        return full

    updates, starts = [], []
    kernels = half % LANES == 0 and features.shape[0] % CHUNK == 0 and feat_width % LANES == 0
    if kernels:
        term, kept, *halves = first_projection(features, residual, 1 - inner_id)
    else:
        halves = [
            lax.dynamic_slice_in_dim(residual, s * half, half, 1).T
            for s in (1 - inner_id, inner_id)
        ]
    lead = 1 - inner_id
    for visit in range(blocks):
        front = (block_id - visit) % blocks
        away, home = halves
        if visit > 0 or not kernels:
            term = project(away.astype(BF16)).astype(BF16)
            kept = project(home.astype(BF16))
        arrived = lax.ppermute(term, "rows", partner)
        if visit == 0:
            inverse_high, inverse_low = split_high_low(inverse_grams)
            turned = turn(features) if kernels else features.T
            arrived, kept, inverse_high, inverse_low = lax.optimization_barrier(
                (arrived, kept, inverse_high, inverse_low)
            )
        else:
            arrived, kept = lax.optimization_barrier((arrived, kept))
        total = kept + arrived.astype(F32)
        update_home = gather_outer(apply_inverse(reduce_outer(total), inverse_high, inverse_low))
        update_away = lax.ppermute(update_home, "rows", partner)
        home = subtract(home, update_home)
        away = subtract(away, update_away)
        updates += [update_home, update_away]
        starts += [front * inner + (1 - lead), front * inner + lead]
        halves = [lax.ppermute(part.astype(BF16), "feat", next_block) for part in (home, away)]
        lead = 1 - lead
    if kernels:
        increments = scatter_rows(updates, starts)
    else:
        increments = jnp.zeros((width * blocks, feat_width), BF16)
        for update, start in zip(updates, starts):
            increments = lax.dynamic_update_slice_in_dim(increments, update, start * half, 0)
    if kernels:
        final = place_columns(halves[0], lead, None)
        return increments, place_columns(halves[1], 1 - lead, final)
    first = jnp.where(lead == 0, halves[0], halves[1])
    second = jnp.where(lead == 0, halves[1], halves[0])
    return increments, jnp.concatenate([first, second], 0).astype(F32).T


def solution(mesh):
    placed = (P("rows", "feat"), P("rows", "feat"), P("feat", None))
    return jax.shard_map(
        on_device,
        mesh=mesh,
        in_specs=placed,
        out_specs=(P(None, "feat"), P("rows", "feat")),
        check_vma=False,
    )
```

```python
import functools

import jax
import jax.numpy as jnp
from jax import lax
from jax.experimental import pallas as pl
from jax.experimental.pallas import tpu as pltpu
from jax.sharding import PartitionSpec as P

BF16 = jnp.bfloat16
F32 = jnp.float32


def split_high_low(value):
    high = lax.reduce_precision(value, 8, 7)
    return high.astype(BF16), (value - high).astype(BF16)


CHUNK = 1024
LANES = 128
TURN_CHUNK = 512
FIRST_VMEM = 56 * 1024 * 1024
SCATTER_VMEM = 12 * 1024 * 1024


def first_kernel(lead_ref, away_ref, home_ref, x_ref, term_ref, kept_ref, away_out, home_out, acc):
    step = pl.program_id(0)
    half = away_ref.shape[1]
    away = away_ref[...].T
    home = home_ref[...].T
    away_out[...] = away
    home_out[...] = home
    both = jnp.concatenate([away, home], 0).astype(BF16)
    product = jnp.dot(both, x_ref[...], preferred_element_type=F32)

    @pl.when(step == 0)
    def _():
        acc[...] = product

    @pl.when(step > 0)
    def _():
        acc[...] += product

    @pl.when(step == pl.num_programs(0) - 1)
    def _():
        term_ref[...] = acc[:half, :].astype(BF16)
        kept_ref[...] = acc[half:, :]


def first_projection(features, residual, lead):
    rows, feat_width = features.shape
    half = residual.shape[1] // 2
    return pl.pallas_call(
        first_kernel,
        out_shape=(
            jax.ShapeDtypeStruct((half, feat_width), BF16),
            jax.ShapeDtypeStruct((half, feat_width), F32),
            jax.ShapeDtypeStruct((half, rows), F32),
            jax.ShapeDtypeStruct((half, rows), F32),
        ),
        grid_spec=pltpu.PrefetchScalarGridSpec(
            num_scalar_prefetch=1,
            grid=(rows // CHUNK,),
            in_specs=[
                pl.BlockSpec((CHUNK, half), lambda i, lead: (i, lead[0])),
                pl.BlockSpec((CHUNK, half), lambda i, lead: (i, 1 - lead[0])),
                pl.BlockSpec((CHUNK, feat_width), lambda i, lead: (i, 0)),
            ],
            out_specs=[
                pl.BlockSpec((half, feat_width), lambda i, lead: (0, 0)),
                pl.BlockSpec((half, feat_width), lambda i, lead: (0, 0)),
                pl.BlockSpec((half, CHUNK), lambda i, lead: (0, i)),
                pl.BlockSpec((half, CHUNK), lambda i, lead: (0, i)),
            ],
            scratch_shapes=[pltpu.VMEM((2 * half, feat_width), F32)],
        ),
        compiler_params=pltpu.CompilerParams(vmem_limit_bytes=FIRST_VMEM),
        cost_estimate=pl.CostEstimate(
            flops=4 * rows * half * feat_width,
            bytes_accessed=2 * rows * feat_width + 16 * rows * half + 6 * half * feat_width,
            transcendentals=0,
        ),
    )(lead.reshape(1), residual, residual, features)


def turn_kernel(x_ref, out_ref):
    out_ref[...] = x_ref[...].T


def turn(features):
    rows, feat_width = features.shape
    return pl.pallas_call(
        turn_kernel,
        out_shape=jax.ShapeDtypeStruct((feat_width, rows), features.dtype),
        grid=(rows // TURN_CHUNK,),
        in_specs=[pl.BlockSpec((TURN_CHUNK, feat_width), lambda i: (i, 0))],
        out_specs=pl.BlockSpec((feat_width, TURN_CHUNK), lambda i: (0, i)),
        compiler_params=pltpu.CompilerParams(vmem_limit_bytes=SCATTER_VMEM),
        cost_estimate=pl.CostEstimate(
            flops=0, bytes_accessed=4 * rows * feat_width, transcendentals=0
        ),
    )(features)


def scatter_kernel(pieces, start_ref, *refs):
    updates, out_ref = refs[:pieces], refs[pieces]
    height = updates[0].shape[0]
    for at in range(pieces):
        rows = pl.ds(pl.multiple_of(start_ref[at] * height, height), height)
        out_ref[rows, :] = updates[at][...]


def scatter_rows(updates, starts):
    pieces = len(updates)
    height, feat_width = updates[0].shape
    whole = lambda i, starts: (0, 0)
    return pl.pallas_call(
        functools.partial(scatter_kernel, pieces),
        out_shape=jax.ShapeDtypeStruct((pieces * height, feat_width), BF16),
        grid_spec=pltpu.PrefetchScalarGridSpec(
            num_scalar_prefetch=1,
            grid=(1,),
            in_specs=[pl.BlockSpec((height, feat_width), whole)] * pieces,
            out_specs=pl.BlockSpec((pieces * height, feat_width), whole),
        ),
        compiler_params=pltpu.CompilerParams(vmem_limit_bytes=FIRST_VMEM),
        cost_estimate=pl.CostEstimate(
            flops=0, bytes_accessed=4 * pieces * height * feat_width, transcendentals=0
        ),
    )(jnp.stack(starts).astype(jnp.int32), *updates)


def place_kernel(place_ref, part_ref, *refs):
    refs[-1][...] = part_ref[...].astype(F32).T


def place_columns(part, place, base):
    half, rows = part.shape
    operands = (part,) if base is None else (part, base)
    in_specs = [pl.BlockSpec((half, CHUNK), lambda i, place: (0, i))]
    if base is not None:
        in_specs.append(pl.BlockSpec(memory_space=pl.ANY))
    return pl.pallas_call(
        place_kernel,
        out_shape=jax.ShapeDtypeStruct((rows, 2 * half), F32),
        grid_spec=pltpu.PrefetchScalarGridSpec(
            num_scalar_prefetch=1,
            grid=(rows // CHUNK,),
            in_specs=in_specs,
            out_specs=pl.BlockSpec((CHUNK, half), lambda i, place: (i, place[0])),
        ),
        input_output_aliases={} if base is None else {2: 0},
        compiler_params=pltpu.CompilerParams(vmem_limit_bytes=SCATTER_VMEM),
        cost_estimate=pl.CostEstimate(
            flops=0, bytes_accessed=6 * rows * half, transcendentals=0
        ),
    )(place.reshape(1).astype(jnp.int32), *operands)


def on_device(features, residual, inverse_grams):
    blocks = lax.axis_size("feat")
    block_id = lax.axis_index("feat")
    shards = lax.axis_size("rows")
    shard_id = lax.axis_index("rows")
    width = residual.shape[1]
    feat_width = features.shape[1]
    inner = 2
    outer = shards // inner
    inner_id = shard_id % inner
    outer_id = shard_id // inner
    half = width // inner
    piece = half // outer
    next_block = [(source, (source + 1) % blocks) for source in range(blocks)]
    partner = [(source, source ^ 1) for source in range(shards)]
    outer_groups = [[o * inner + i for o in range(outer)] for i in range(inner)]
    direct = outer == 4

    def outer_step(step):
        return [(o * inner + i, (o ^ step) * inner + i) for o in range(outer) for i in range(inner)]

    def project(current):
        return lax.dot_general(
            current, features, (((1,), (0,)), ((), ())), preferred_element_type=F32
        )

    def apply_inverse(projected, inverse_high, inverse_low):
        high, low = split_high_low(projected)
        dims = (((1,), (1,)), ((), ()))
        dot = lambda a, b: lax.dot_general(a, b, dims, preferred_element_type=F32)
        both = dot(jnp.concatenate([high, low], 0), inverse_high)
        return (both[: high.shape[0]] + both[high.shape[0]:] + dot(high, inverse_low)).astype(BF16)

    def subtract(current, update):
        change = lax.dot_general(
            update, turned, (((1,), (0,)), ((), ())), preferred_element_type=F32
        )
        return current.astype(F32) - change

    def reduce_outer(total):
        if not direct:
            parts = lax.all_to_all(
                total.astype(BF16), "rows", 0, 0, tiled=True, axis_index_groups=outer_groups
            )
            return jnp.sum(parts.reshape(outer, piece, feat_width).astype(F32), axis=0)
        parts = [lax.dynamic_slice_in_dim(total, outer_id * piece, piece, 0)]
        for step in range(outer - 1, 0, -1):
            out = lax.dynamic_slice_in_dim(total, (outer_id ^ step) * piece, piece, 0)
            parts.append(lax.ppermute(out.astype(BF16), "rows", outer_step(step)).astype(F32))
        return sum(parts[1:], parts[0])

    def gather_outer(update):
        if not direct:
            repeated = jnp.concatenate([update] * outer, 0)
            return lax.all_to_all(
                repeated, "rows", 0, 0, tiled=True, axis_index_groups=outer_groups
            )
        full = jnp.zeros((half, feat_width), BF16)
        full = lax.dynamic_update_slice_in_dim(full, update, outer_id * piece, 0)
        for step in range(outer - 1, 0, -1):
            got = lax.ppermute(update, "rows", outer_step(step))
            full = lax.dynamic_update_slice_in_dim(full, got, (outer_id ^ step) * piece, 0)
        return full

    updates, starts = [], []
    kernels = half % LANES == 0 and features.shape[0] % CHUNK == 0 and feat_width % LANES == 0
    if kernels:
        term, kept, *halves = first_projection(features, residual, 1 - inner_id)
    else:
        halves = [
            lax.dynamic_slice_in_dim(residual, s * half, half, 1).T
            for s in (1 - inner_id, inner_id)
        ]
    lead = 1 - inner_id
    for visit in range(blocks):
        front = (block_id - visit) % blocks
        away, home = halves
        if visit > 0 or not kernels:
            term = project(away.astype(BF16)).astype(BF16)
            kept = project(home.astype(BF16))
        arrived = lax.ppermute(term, "rows", partner)
        if visit == 0:
            inverse_high, inverse_low = split_high_low(inverse_grams)
            turned = turn(features) if kernels else features.T
            arrived, kept, inverse_high, inverse_low = lax.optimization_barrier(
                (arrived, kept, inverse_high, inverse_low)
            )
        else:
            arrived, kept = lax.optimization_barrier((arrived, kept))
        total = kept + arrived.astype(F32)
        update_home = gather_outer(apply_inverse(reduce_outer(total), inverse_high, inverse_low))
        update_away = lax.ppermute(update_home, "rows", partner)
        home = subtract(home, update_home)
        away = subtract(away, update_away)
        updates += [update_home, update_away]
        starts += [front * inner + (1 - lead), front * inner + lead]
        halves = [lax.ppermute(part.astype(BF16), "feat", next_block) for part in (home, away)]
        lead = 1 - lead
    if kernels:
        increments = scatter_rows(updates, starts)
    else:
        increments = jnp.zeros((width * blocks, feat_width), BF16)
        for update, start in zip(updates, starts):
            increments = lax.dynamic_update_slice_in_dim(increments, update, start * half, 0)
    if kernels:
        final = place_columns(halves[0], lead, None)
        return increments, place_columns(halves[1], 1 - lead, final)
    first = jnp.where(lead == 0, halves[0], halves[1])
    second = jnp.where(lead == 0, halves[1], halves[0])
    return increments, jnp.concatenate([first, second], 0).astype(F32).T


def solution(mesh):
    placed = (P("rows", "feat"), P("rows", "feat"), P("feat", None))
    return jax.shard_map(
        on_device,
        mesh=mesh,
        in_specs=placed,
        out_specs=(P(None, "feat"), P("rows", "feat")),
        check_vma=False,
    )
```

```python
import functools

import jax
import jax.numpy as jnp
from jax import lax
from jax.experimental import pallas as pl
from jax.experimental.pallas import tpu as pltpu
from jax.sharding import PartitionSpec as P

BF16 = jnp.bfloat16
F32 = jnp.float32


def split_high_low(value):
    high = lax.reduce_precision(value, 8, 7)
    return high.astype(BF16), (value - high).astype(BF16)


CHUNK = 1024
LANES = 128
COLUMNS = 512
TURN_CHUNK = 512
FIRST_VMEM = 56 * 1024 * 1024
SCATTER_VMEM = 12 * 1024 * 1024


def first_kernel(lead_ref, away_ref, home_ref, x_ref, term_ref, kept_ref, away_out, home_out, both):
    half = away_ref.shape[1]

    @pl.when(pl.program_id(0) == 0)
    def _():
        away = away_ref[...].T
        home = home_ref[...].T
        away_out[...] = away
        home_out[...] = home
        both[:half, :] = away.astype(BF16)
        both[half:, :] = home.astype(BF16)

    product = jnp.dot(both[...], x_ref[...], preferred_element_type=F32)
    term_ref[...] = product[:half, :].astype(BF16)
    kept_ref[...] = product[half:, :]


def first_projection(features, residual, lead):
    rows, feat_width = features.shape
    half = residual.shape[1] // 2
    return pl.pallas_call(
        first_kernel,
        out_shape=(
            jax.ShapeDtypeStruct((half, feat_width), BF16),
            jax.ShapeDtypeStruct((half, feat_width), F32),
            jax.ShapeDtypeStruct((half, rows), F32),
            jax.ShapeDtypeStruct((half, rows), F32),
        ),
        grid_spec=pltpu.PrefetchScalarGridSpec(
            num_scalar_prefetch=1,
            grid=(feat_width // COLUMNS,),
            in_specs=[
                pl.BlockSpec((rows, half), lambda i, lead: (0, lead[0])),
                pl.BlockSpec((rows, half), lambda i, lead: (0, 1 - lead[0])),
                pl.BlockSpec((rows, COLUMNS), lambda i, lead: (0, i)),
            ],
            out_specs=[
                pl.BlockSpec((half, COLUMNS), lambda i, lead: (0, i)),
                pl.BlockSpec((half, COLUMNS), lambda i, lead: (0, i)),
                pl.BlockSpec((half, rows), lambda i, lead: (0, 0)),
                pl.BlockSpec((half, rows), lambda i, lead: (0, 0)),
            ],
            scratch_shapes=[pltpu.VMEM((2 * half, rows), BF16)],
        ),
        compiler_params=pltpu.CompilerParams(vmem_limit_bytes=FIRST_VMEM),
        cost_estimate=pl.CostEstimate(
            flops=4 * rows * half * feat_width,
            bytes_accessed=2 * rows * feat_width + 16 * rows * half + 6 * half * feat_width,
            transcendentals=0,
        ),
    )(lead.reshape(1), residual, residual, features)


def turn_kernel(x_ref, out_ref):
    out_ref[...] = x_ref[...].T


def turn(features):
    rows, feat_width = features.shape
    return pl.pallas_call(
        turn_kernel,
        out_shape=jax.ShapeDtypeStruct((feat_width, rows), features.dtype),
        grid=(rows // TURN_CHUNK,),
        in_specs=[pl.BlockSpec((TURN_CHUNK, feat_width), lambda i: (i, 0))],
        out_specs=pl.BlockSpec((feat_width, TURN_CHUNK), lambda i: (0, i)),
        compiler_params=pltpu.CompilerParams(vmem_limit_bytes=SCATTER_VMEM),
        cost_estimate=pl.CostEstimate(
            flops=0, bytes_accessed=4 * rows * feat_width, transcendentals=0
        ),
    )(features)


def scatter_kernel(pieces, start_ref, *refs):
    updates, out_ref = refs[:pieces], refs[pieces]
    height = updates[0].shape[0]
    for at in range(pieces):
        rows = pl.ds(pl.multiple_of(start_ref[at] * height, height), height)
        out_ref[rows, :] = updates[at][...]


def scatter_rows(updates, starts):
    pieces = len(updates)
    height, feat_width = updates[0].shape
    whole = lambda i, starts: (0, 0)
    return pl.pallas_call(
        functools.partial(scatter_kernel, pieces),
        out_shape=jax.ShapeDtypeStruct((pieces * height, feat_width), BF16),
        grid_spec=pltpu.PrefetchScalarGridSpec(
            num_scalar_prefetch=1,
            grid=(1,),
            in_specs=[pl.BlockSpec((height, feat_width), whole)] * pieces,
            out_specs=pl.BlockSpec((pieces * height, feat_width), whole),
        ),
        compiler_params=pltpu.CompilerParams(vmem_limit_bytes=FIRST_VMEM),
        cost_estimate=pl.CostEstimate(
            flops=0, bytes_accessed=4 * pieces * height * feat_width, transcendentals=0
        ),
    )(jnp.stack(starts).astype(jnp.int32), *updates)


def place_kernel(place_ref, part_ref, *refs):
    refs[-1][...] = part_ref[...].astype(F32).T


def place_columns(part, place, base):
    half, rows = part.shape
    operands = (part,) if base is None else (part, base)
    in_specs = [pl.BlockSpec((half, CHUNK), lambda i, place: (0, i))]
    if base is not None:
        in_specs.append(pl.BlockSpec(memory_space=pl.ANY))
    return pl.pallas_call(
        place_kernel,
        out_shape=jax.ShapeDtypeStruct((rows, 2 * half), F32),
        grid_spec=pltpu.PrefetchScalarGridSpec(
            num_scalar_prefetch=1,
            grid=(rows // CHUNK,),
            in_specs=in_specs,
            out_specs=pl.BlockSpec((CHUNK, half), lambda i, place: (i, place[0])),
        ),
        input_output_aliases={} if base is None else {2: 0},
        compiler_params=pltpu.CompilerParams(vmem_limit_bytes=SCATTER_VMEM),
        cost_estimate=pl.CostEstimate(
            flops=0, bytes_accessed=6 * rows * half, transcendentals=0
        ),
    )(place.reshape(1).astype(jnp.int32), *operands)


def on_device(features, residual, inverse_grams):
    blocks = lax.axis_size("feat")
    block_id = lax.axis_index("feat")
    shards = lax.axis_size("rows")
    shard_id = lax.axis_index("rows")
    width = residual.shape[1]
    feat_width = features.shape[1]
    inner = 2
    outer = shards // inner
    inner_id = shard_id % inner
    outer_id = shard_id // inner
    half = width // inner
    piece = half // outer
    next_block = [(source, (source + 1) % blocks) for source in range(blocks)]
    partner = [(source, source ^ 1) for source in range(shards)]
    outer_groups = [[o * inner + i for o in range(outer)] for i in range(inner)]
    direct = outer == 4

    def outer_step(step):
        return [(o * inner + i, (o ^ step) * inner + i) for o in range(outer) for i in range(inner)]

    def project(current):
        return lax.dot_general(
            current, features, (((1,), (0,)), ((), ())), preferred_element_type=F32
        )

    def apply_inverse(projected, inverse_high, inverse_low):
        high, low = split_high_low(projected)
        dims = (((1,), (1,)), ((), ()))
        dot = lambda a, b: lax.dot_general(a, b, dims, preferred_element_type=F32)
        both = dot(jnp.concatenate([high, low], 0), inverse_high)
        return (both[: high.shape[0]] + both[high.shape[0]:] + dot(high, inverse_low)).astype(BF16)

    def subtract(current, update):
        change = lax.dot_general(
            update, turned, (((1,), (0,)), ((), ())), preferred_element_type=F32
        )
        return current.astype(F32) - change

    def reduce_outer(total):
        if not direct:
            parts = lax.all_to_all(
                total.astype(BF16), "rows", 0, 0, tiled=True, axis_index_groups=outer_groups
            )
            return jnp.sum(parts.reshape(outer, piece, feat_width).astype(F32), axis=0)
        parts = [lax.dynamic_slice_in_dim(total, outer_id * piece, piece, 0)]
        for step in range(outer - 1, 0, -1):
            out = lax.dynamic_slice_in_dim(total, (outer_id ^ step) * piece, piece, 0)
            parts.append(lax.ppermute(out.astype(BF16), "rows", outer_step(step)).astype(F32))
        return sum(parts[1:], parts[0])

    def gather_outer(update):
        if not direct:
            repeated = jnp.concatenate([update] * outer, 0)
            return lax.all_to_all(
                repeated, "rows", 0, 0, tiled=True, axis_index_groups=outer_groups
            )
        full = jnp.zeros((half, feat_width), BF16)
        full = lax.dynamic_update_slice_in_dim(full, update, outer_id * piece, 0)
        for step in range(outer - 1, 0, -1):
            got = lax.ppermute(update, "rows", outer_step(step))
            full = lax.dynamic_update_slice_in_dim(full, got, (outer_id ^ step) * piece, 0)
        return full

    updates, starts = [], []
    kernels = half % LANES == 0 and features.shape[0] % CHUNK == 0 and feat_width % COLUMNS == 0
    if kernels:
        term, kept, *halves = first_projection(features, residual, 1 - inner_id)
    else:
        halves = [
            lax.dynamic_slice_in_dim(residual, s * half, half, 1).T
            for s in (1 - inner_id, inner_id)
        ]
    lead = 1 - inner_id
    for visit in range(blocks):
        front = (block_id - visit) % blocks
        away, home = halves
        if visit > 0 or not kernels:
            term = project(away.astype(BF16)).astype(BF16)
            kept = project(home.astype(BF16))
        arrived = lax.ppermute(term, "rows", partner)
        if visit == 0:
            inverse_high, inverse_low = split_high_low(inverse_grams)
            turned = turn(features) if kernels else features.T
            arrived, kept, inverse_high, inverse_low = lax.optimization_barrier(
                (arrived, kept, inverse_high, inverse_low)
            )
        else:
            arrived, kept = lax.optimization_barrier((arrived, kept))
        total = kept + arrived.astype(F32)
        update_home = gather_outer(apply_inverse(reduce_outer(total), inverse_high, inverse_low))
        update_away = lax.ppermute(update_home, "rows", partner)
        home = subtract(home, update_home)
        away = subtract(away, update_away)
        updates += [update_home, update_away]
        starts += [front * inner + (1 - lead), front * inner + lead]
        halves = [lax.ppermute(part.astype(BF16), "feat", next_block) for part in (home, away)]
        lead = 1 - lead
    if kernels:
        increments = scatter_rows(updates, starts)
    else:
        increments = jnp.zeros((width * blocks, feat_width), BF16)
        for update, start in zip(updates, starts):
            increments = lax.dynamic_update_slice_in_dim(increments, update, start * half, 0)
    if kernels:
        final = place_columns(halves[0], lead, None)
        return increments, place_columns(halves[1], 1 - lead, final)
    first = jnp.where(lead == 0, halves[0], halves[1])
    second = jnp.where(lead == 0, halves[1], halves[0])
    return increments, jnp.concatenate([first, second], 0).astype(F32).T


def solution(mesh):
    placed = (P("rows", "feat"), P("rows", "feat"), P("feat", None))
    return jax.shard_map(
        on_device,
        mesh=mesh,
        in_specs=placed,
        out_specs=(P(None, "feat"), P("rows", "feat")),
        check_vma=False,
    )
```
